32 devices in a mesh: dp: 4 (over y, x), fetch: 8 (over z, core).
Axes of the slice: x: 2, y: 2, z: 4, core: 2. Of those that a mesh axis runs over, the one named last changes fastest.
Arguments:
- tokens: bfloat16 [4096, 6144], P(('dp', 'fetch')), may hold values from -6 to 6
- routes: int32 [4096, 2], P(('dp', 'fetch')), may hold values from 0 to 7, as said below
- route_probs: float32 [4096, 2], P(('dp', 'fetch')), may hold values from 0.1 to 1
- gate_weight: bfloat16 [6144, 8192], P(None, 'fetch'), may hold values from -0.078125 to 0.078125
- up_weight: bfloat16 [6144, 8192], P(None, 'fetch'), may hold values from -0.078125 to 0.078125
- down_weight: bfloat16 [8192, 6144], P('fetch'), may hold values from -0.0625 to 0.0625
- out_grad: bfloat16 [4096, 6144], P(('dp', 'fetch')), may hold values from -6 to 6
Outputs:
- token_grad: bfloat16 [4096, 6144], P(('dp', 'fetch'))
- gate_grad: bfloat16 [6144, 8192], P('dp', 'fetch')
- up_grad: bfloat16 [6144, 8192], P('dp', 'fetch')
- down_grad: bfloat16 [8192, 6144], P('fetch', 'dp')
The draws below stay inside these ranges and needn't reach their ends.
Inputs may be any that keep to these rules, and one draw needn't show every extreme that they name: `routes`: the two numbers of a row differ. In every aligned block of 128 rows (the rows of one device) between 16 and 32 rows name expert 0, and one block in every draw has exactly 32 of them.
All inputs are finite; a program needn't handle non-finite values.
Results may differ from the reference program's by a relative error of at most 0.023.
Values may be sent and summed in bfloat16 or wider, within the bound.
No kernel may reach another device: no remote copies, remote signals or barrier semaphores. Data moves between devices by JAX's collectives and lax.ppermute only.
A program may use at most 192 MiB of HBM per device.

```python
import jax
import jax.numpy as jnp
from jax import lax

D = 6144
EXPERTS = 8
TOP = 2
FF_WIN = 8192
TOK_DEV = 128
CAP = 32
TOKENS = 4096
SLAB = 1024
GROUP = 256
N_DP = 4
N_FETCH = 8


def draw_routes(key, part):
    key = jax.random.fold_in(key, 11)
    keys = jax.random.split(key, 6)
    blocks = TOKENS // TOK_DEV
    counts = jax.random.randint(keys[0], (blocks,), CAP // 2, CAP + 1)
    fullest = jax.random.randint(keys[1], (), 0, blocks)
    counts = jnp.where(jnp.arange(blocks) == fullest, CAP, counts)
    scores = jax.random.randint(keys[2], (blocks, TOK_DEV), 0, 2 ** 20) * TOK_DEV + jnp.arange(TOK_DEV)[None, :]
    ranks = jnp.argsort(jnp.argsort(scores, axis=1), axis=1)
    routed = ranks < counts[:, None]
    position = jax.random.randint(keys[3], (blocks, TOK_DEV), 0, 2)
    first_other = jax.random.randint(keys[4], (blocks, TOK_DEV), 1, EXPERTS)
    second_other = jax.random.randint(keys[5], (blocks, TOK_DEV), 1, EXPERTS - 1)
    second_other = jnp.where(second_other >= first_other, second_other + 1, second_other)
    leading = jnp.where(routed, 0, first_other)
    slot_zero = jnp.where(position == 0, leading, second_other)
    slot_one = jnp.where(position == 0, second_other, leading)
    return jnp.stack([slot_zero, slot_one], axis=-1).reshape(TOKENS, TOP).astype(jnp.int32)


def block_scale(stream_key, shape, pieces, least, high):
    loudness, own = 1.0, jax.random.fold_in(stream_key, 6)
    for dim, parts in pieces:
        heights = jnp.exp(jax.random.uniform(jax.random.fold_in(own, dim), (parts,), jnp.float32, least / len(pieces), high / len(pieces)))
        loudness = loudness * jnp.repeat(heights, shape[dim] // parts).reshape([-1 if axis == dim else 1 for axis in range(len(shape))])
    return loudness


def scatter_about(stream_key, extent, deviation, limit, cuts=(), kind=jnp.bfloat16):
    result = deviation * jax.random.normal(stream_key, extent, jnp.float32)
    if cuts:
        result = result * block_scale(stream_key, extent, cuts, -0.22, 0.18)
    return jnp.clip(result, -limit, limit).astype(kind)


def setup_inputs(seed: int = 0) -> dict:
    streams_of = jax.random.split(jax.random.key(seed), 8)
    tokens = scatter_about(streams_of[0], (TOKENS, D), 1.0, 6.0, ((0, 32),))
    routes = draw_routes(jax.random.fold_in(streams_of[7], 71), 0)
    route_probs = jnp.clip(0.1 + 0.9 * jax.random.uniform(streams_of[2], (TOKENS, TOP), jnp.float32) ** block_scale(streams_of[2], (TOKENS, TOP), ((0, 32),), -0.2, 0.2), 0.1, 1.0)
    gate_weight = scatter_about(streams_of[3], (D, FF_WIN), D ** -0.5, 0.078125, ((1, 8),))
    up_weight = scatter_about(streams_of[4], (D, FF_WIN), D ** -0.5, 0.078125, ((1, 8),))
    down_weight = scatter_about(streams_of[5], (FF_WIN, D), FF_WIN ** -0.5, 0.0625, ((0, 8),))
    out_grad = scatter_about(streams_of[6], (TOKENS, D), 1.0, 6.0, ((0, 32),))
    return dict(tokens=tokens, routes=routes, route_probs=route_probs, gate_weight=gate_weight, up_weight=up_weight, down_weight=down_weight, out_grad=out_grad)


def settle(value):
    return lax.optimization_barrier(value.astype(jnp.bfloat16)).astype(jnp.float32)


def reference(tokens, routes, route_probs, gate_weight, up_weight, down_weight, out_grad):
    blocks = TOKENS // TOK_DEV
    hits = routes == 0
    coef = jnp.sum(jnp.where(hits, route_probs, jnp.float32(0.0)), axis=1)
    keyed = jnp.where(jnp.any(hits, axis=1), 0, 1).astype(jnp.int32).reshape(blocks, TOK_DEV)
    order = jnp.argsort(keyed, axis=1, stable=True)[:, :CAP].astype(jnp.int32)
    slots = (order + (jnp.arange(blocks, dtype=jnp.int32) * TOK_DEV)[:, None]).reshape(-1).astype(jnp.int32)
    picked = tokens[slots]
    scaled = (coef[slots][:, None] * out_grad[slots].astype(jnp.float32)).astype(jnp.bfloat16)
    gate = jnp.dot(picked, gate_weight, preferred_element_type=jnp.float32)
    up = jnp.dot(picked, up_weight, preferred_element_type=jnp.float32)
    sig = jax.nn.sigmoid(gate)
    act = gate * sig
    hidden = (act * up).astype(jnp.bfloat16)
    hidden_grad = jnp.dot(scaled, down_weight.T, preferred_element_type=jnp.float32)
    up_rows = (hidden_grad * act).astype(jnp.bfloat16)
    gate_rows = (hidden_grad * up * sig * (1.0 + gate * (1.0 - sig))).astype(jnp.bfloat16)
    input_rows = jnp.zeros((slots.shape[0], D), jnp.float32)
    for slab in range(N_FETCH):
        lo = slab * SLAB
        term = jnp.dot(gate_rows[:, lo:lo + SLAB], gate_weight[:, lo:lo + SLAB].T, preferred_element_type=jnp.float32)
        term = term + jnp.dot(up_rows[:, lo:lo + SLAB], up_weight[:, lo:lo + SLAB].T, preferred_element_type=jnp.float32)
        input_rows = input_rows + settle(term)
    token_grad = jnp.zeros((TOKENS, D), jnp.bfloat16).at[slots].set(input_rows.astype(jnp.bfloat16))
    gate_total = jnp.zeros((D, FF_WIN), jnp.float32)
    up_total = jnp.zeros((D, FF_WIN), jnp.float32)
    down_total = jnp.zeros((FF_WIN, D), jnp.float32)
    for group in range(N_DP):
        lo = group * GROUP
        rows_part = picked[lo:lo + GROUP]
        gate_total = gate_total + settle(jnp.dot(rows_part.T, gate_rows[lo:lo + GROUP], preferred_element_type=jnp.float32))
        up_total = up_total + settle(jnp.dot(rows_part.T, up_rows[lo:lo + GROUP], preferred_element_type=jnp.float32))
        down_total = down_total + settle(jnp.dot(hidden[lo:lo + GROUP].T, scaled[lo:lo + GROUP], preferred_element_type=jnp.float32))
    return token_grad, gate_total.astype(jnp.bfloat16), up_total.astype(jnp.bfloat16), down_total.astype(jnp.bfloat16)
```

```python
import functools

import jax
import jax.numpy as jnp
from jax import lax
from jax.experimental import pallas as pl
from jax.experimental.pallas import tpu as pltpu
from jax.sharding import PartitionSpec as P

CAP = 32
F32, BF16 = jnp.float32, jnp.bfloat16
ROWS = (((0,), (0,)), ((), ()))
LAST = (((1,), (1,)), ((), ()))
VMEM = pl.BlockSpec(memory_space=pltpu.VMEM)


def mm(a, b, dims=(((1,), (0,)), ((), ()))):
    return lax.dot_general(a, b, dims, preferred_element_type=F32)


def pick_kernel(routes, probs, tokens, out_grad, sel_out, picked, scaled):
    n = tokens.shape[0]
    hits = routes[...] == 0
    coef = jnp.sum(jnp.where(hits, probs[...], 0.0), axis=0, keepdims=True)
    routed = jnp.sum(jnp.where(hits, 1.0, 0.0), axis=0, keepdims=True) > 0.5
    flags = jnp.broadcast_to(jnp.where(routed, 1.0, 0.0), (8, n))
    before = lax.broadcasted_iota(jnp.int32, (n, n), 0) <= lax.broadcasted_iota(jnp.int32, (n, n), 1)
    upto = mm(flags.astype(BF16), jnp.where(before, 1.0, 0.0).astype(BF16))[:1]
    count = jnp.sum(flags[:1], axis=1, keepdims=True)
    lane = lax.broadcasted_iota(jnp.int32, (1, n), 1).astype(F32)
    rank = jnp.where(routed, upto - 1.0, count + lane - upto)
    sel = rank == lax.broadcasted_iota(jnp.int32, (CAP, n), 0).astype(F32)
    scale = jnp.sum(jnp.where(sel, coef, 0.0), axis=1, keepdims=True)
    sel = jnp.where(sel, 1.0, 0.0).astype(BF16)
    sel_out[...] = sel
    picked[...] = mm(sel, tokens[...]).astype(BF16)
    scaled[...] = (scale * mm(sel, out_grad[...])).astype(BF16)


def pick(tokens, routes, probs, out_grad):
    d = tokens.shape[1]
    rows = jax.ShapeDtypeStruct((CAP, d), BF16)
    return pl.pallas_call(
        pick_kernel,
        out_shape=(jax.ShapeDtypeStruct((CAP, tokens.shape[0]), BF16), rows, rows),
        in_specs=[VMEM] * 4,
        out_specs=(VMEM,) * 3,
        compiler_params=pltpu.CompilerParams(vmem_limit_bytes=32 << 20),
    )(routes.T, probs.T, tokens, out_grad)


def put_kernel(sel, *refs):
    *parts, out = refs
    total = parts[0][...].astype(F32)
    for part in parts[1:]:
        total = total + part[...].astype(F32)
    out[...] = mm(sel[...], total.astype(BF16), ROWS).astype(BF16)


def put(sel, parts):
    d = parts[0].shape[1]
    return pl.pallas_call(
        put_kernel,
        out_shape=jax.ShapeDtypeStruct((sel.shape[1], d), BF16),
        in_specs=[VMEM] * (1 + len(parts)),
        out_specs=VMEM,
        compiler_params=pltpu.CompilerParams(vmem_limit_bytes=32 << 20),
    )(sel, *parts)


def on_device(tokens, routes, route_probs, gate_weight, up_weight, down_weight, out_grad):
    n_dp, n_fetch = lax.axis_size("dp"), lax.axis_size("fetch")
    chips = n_fetch // 2

    def move(x, hop):
        pairs = [(2 * z + c, 2 * ((z + hop) % chips) + c) for z in range(chips) for c in range(2)]
        return lax.ppermute(x, "fetch", pairs)

    def swap(x):
        return lax.ppermute(x, "fetch", [(k, k ^ 1) for k in range(n_fetch)])

    def across(x, bits):
        return lax.ppermute(x, "dp", [(k, k ^ bits) for k in range(n_dp)])

    offsets = [0]
    for s in range(1, chips // 2 + 1):
        offsets += [-s] if 2 * s == chips else [-s, s]

    def ring(x):
        blocks = {0: x}
        for s in range(1, chips // 2 + 1):
            blocks[-s] = move(blocks[1 - s], 1)
            if 2 * s != chips:
                blocks[s] = move(blocks[s - 1], -1)
        mine = jnp.concatenate([blocks[o] for o in offsets])
        return mine, swap(mine)

    def spread(x):
        if n_dp != 4:
            return lax.all_gather(x, "dp", axis=0, tiled=True)
        half = x.shape[0] // 2
        by_x, by_y = across(x, 1), across(x, 2)
        far = [across(by_x[:half], 2), across(by_y[half:], 1)]
        return jnp.concatenate([x, by_x, by_y] + far)

    def slices(x):
        width = x.shape[1] // n_dp
        if n_dp != 4:
            got = lax.all_to_all(x, "dp", 1, 0, tiled=True)
            got = got.reshape(n_dp, -1, width)
        else:
            me = lax.axis_index("dp")
            cut = [lax.dynamic_slice_in_dim(x, (me ^ k) * width, width, 1) for k in range(4)]
            got = jnp.stack([cut[0]] + [across(cut[k], k) for k in range(1, 4)])
        return jnp.concatenate([got, swap(got)], axis=1).reshape(-1, width)

    sel, picked, scaled = pick(tokens, routes, route_probs, out_grad)
    picked_mine, picked_theirs = ring(picked)
    scaled_mine, scaled_theirs = ring(scaled)
    rows = jnp.concatenate([picked_mine, picked_theirs])
    grads = jnp.concatenate([scaled_mine, scaled_theirs])
    picked_slices = slices(picked_mine)
    scaled_slices = slices(scaled_mine)

    gate = mm(rows, gate_weight)
    up = mm(rows, up_weight)
    sig = jax.nn.sigmoid(gate)
    act = gate * sig
    hidden = spread((act * up).astype(BF16))
    hidden_grad = mm(grads, down_weight, LAST)
    up_rows = (hidden_grad * act).astype(BF16)
    gate_rows = (hidden_grad * up * sig * (1.0 + gate * (1.0 - sig))).astype(BF16)
    gate_all, up_all = spread(gate_rows), spread(up_rows)

    term = (mm(gate_rows, gate_weight, LAST) + mm(up_rows, up_weight, LAST)).astype(BF16)
    half = CAP * chips
    term = (term[:half].astype(F32) + swap(term[half:]).astype(F32)).astype(BF16)
    parts = [term[:CAP]]
    for k, o in enumerate(offsets[1:], 1):
        parts.append(move(term[k * CAP : (k + 1) * CAP], o))
    token_grad = put(sel, parts)

    down_grad = mm(hidden, scaled_slices, ROWS).astype(BF16)
    gate_grad = mm(picked_slices, gate_all, ROWS).astype(BF16)
    up_grad = mm(picked_slices, up_all, ROWS).astype(BF16)
    return token_grad, gate_grad, up_grad, down_grad


def solution(mesh):
    return jax.shard_map(
        on_device,
        mesh=mesh,
        in_specs=(
            P(("dp", "fetch"), None),
            P(("dp", "fetch"), None),
            P(("dp", "fetch"), None),
            P(None, "fetch"),
            P(None, "fetch"),
            P("fetch", None),
            P(("dp", "fetch"), None),
        ),
        out_specs=(P(("dp", "fetch"), None), P("dp", "fetch"), P("dp", "fetch"), P("fetch", "dp")),
        check_vma=False,
    )
```

```python
import functools

import jax
import jax.numpy as jnp
from jax import lax
from jax.experimental import pallas as pl
from jax.experimental.pallas import tpu as pltpu
from jax.sharding import PartitionSpec as P

CAP = 32
F32, BF16 = jnp.float32, jnp.bfloat16
ROWS = (((0,), (0,)), ((), ()))
LAST = (((1,), (1,)), ((), ()))
VMEM = pl.BlockSpec(memory_space=pltpu.VMEM)
SMEM = pl.BlockSpec(memory_space=pltpu.SMEM)
ANY = pl.BlockSpec(memory_space=pl.ANY)
LIMIT = 40 << 20


def mm(a, b, dims=(((1,), (0,)), ((), ()))):
    return lax.dot_general(a, b, dims, preferred_element_type=F32)


def shape(dims, kind=BF16):
    return jax.ShapeDtypeStruct(tuple(dims), kind)


def params(limit=LIMIT):
    return pltpu.CompilerParams(vmem_limit_bytes=limit)


def cost(flops, nbytes, weigh=64):
    return pl.CostEstimate(flops=int(flops) // weigh, bytes_accessed=int(nbytes) // weigh, transcendentals=0)


def fetch(source, held, sem, parts):
    width = source.shape[1] // parts
    copies = []
    for i in range(parts):
        cols = pl.ds(i * width, width)
        copies.append(pltpu.make_async_copy(source.at[:, cols], held.at[:, cols], sem.at[i]))
        copies[-1].start()
    return copies


def pick_kernel(me, routes, probs, tokens, out_grad, sel_out, both, held, sem):
    _, n_dp, _, width = both.shape
    copies = fetch(tokens, held.at[0], sem.at[0], n_dp) + fetch(out_grad, held.at[1], sem.at[1], n_dp)
    n = tokens.shape[0]
    hits = routes[...] == 0
    coef = jnp.sum(jnp.where(hits, probs[...], 0.0), axis=0, keepdims=True)
    routed = jnp.sum(jnp.where(hits, 1.0, 0.0), axis=0, keepdims=True) > 0.5
    flags = jnp.broadcast_to(jnp.where(routed, 1.0, 0.0), (8, n))
    before = lax.broadcasted_iota(jnp.int32, (n, n), 0) <= lax.broadcasted_iota(jnp.int32, (n, n), 1)
    upto = mm(flags.astype(BF16), jnp.where(before, 1.0, 0.0).astype(BF16))[:1]
    count = jnp.sum(flags[:1], axis=1, keepdims=True)
    lane = lax.broadcasted_iota(jnp.int32, (1, n), 1).astype(F32)
    rank = jnp.where(routed, upto - 1.0, count + lane - upto)
    sel = rank == lax.broadcasted_iota(jnp.int32, (CAP, n), 0).astype(F32)
    scale = jnp.sum(jnp.where(sel, coef, 0.0), axis=1, keepdims=True)
    sel = jnp.where(sel, 1.0, 0.0).astype(BF16)
    sel_out[...] = sel
    for copy in copies:
        copy.wait()
    for k in range(n_dp):
        cols = pl.ds(pl.multiple_of((me[0] ^ k) * width, 128), width)
        both[0, k] = mm(sel, held[0, :, cols]).astype(BF16)
        both[1, k] = (scale * mm(sel, held[1, :, cols])).astype(BF16)


def pick(me, tokens, routes, probs, out_grad, n_dp):
    n, d = tokens.shape
    return pl.pallas_call(
        pick_kernel,
        out_shape=(shape((CAP, n)), shape((2, n_dp, CAP, d // n_dp))),
        in_specs=[SMEM, VMEM, VMEM, ANY, ANY],
        out_specs=(VMEM,) * 2,
        scratch_shapes=[pltpu.VMEM((2, n, d), BF16), pltpu.SemaphoreType.DMA((2, n_dp))],
        compiler_params=params(60 << 20),
        cost_estimate=cost(4 * CAP * n * d, 5 * n * d),
    )(me, routes.T, probs.T, tokens, out_grad)


def after(x, *deps):
    def kernel(*refs):
        del refs

    return pl.pallas_call(
        kernel,
        out_shape=shape(x.shape, x.dtype),
        in_specs=[ANY] * (1 + len(deps)),
        out_specs=ANY,
        input_output_aliases={0: 0},
        compiler_params=params(1 << 20),
        cost_estimate=cost(0, 0),
    )(x, *deps)


def lay_kernel(count, deps, whole, *refs):
    blocks, rest, sem = refs[:count], list(refs[count + deps : -1]), refs[-1]
    copies = []
    at = 0
    for b in blocks:
        rows = pl.ds(at, b.shape[2])
        at += b.shape[2]
        if whole:
            copies.append((b, rest[0].at[:, :, rows]))
        for k, out in enumerate(rest[whole:], 1):
            copies.append((b.at[:, k], out.at[:, rows]))
    copies = [pltpu.make_async_copy(a, b, sem.at[i]) for i, (a, b) in enumerate(copies)]
    for copy in copies:
        copy.start()
    for copy in copies:
        copy.wait()


def lay(blocks, whole, deps=()):
    arrays, slices, _, width = blocks[0].shape
    rows = sum(b.shape[2] for b in blocks)
    outs = [shape((arrays, slices, rows, width))] * whole + [shape((arrays, rows, width))] * (slices - 1)
    return pl.pallas_call(
        functools.partial(lay_kernel, len(blocks), len(deps), whole),
        out_shape=outs,
        in_specs=[ANY] * (len(blocks) + len(deps)),
        out_specs=[ANY] * len(outs),
        scratch_shapes=[pltpu.SemaphoreType.DMA((len(blocks) * (whole + slices - 1),))],
        compiler_params=params(1 << 20),
        cost_estimate=cost(0, 4 * arrays * slices * rows * width),
    )(*blocks, *deps)


def pile_kernel(count, *refs):
    blocks, out, sem = refs[:count], refs[-2], refs[-1]
    copies = [pltpu.make_async_copy(b, out.at[i], sem.at[i]) for i, b in enumerate(blocks)]
    for copy in copies:
        copy.start()
    for copy in copies:
        copy.wait()


def pile(blocks, *deps):
    return pl.pallas_call(
        functools.partial(pile_kernel, len(blocks)),
        out_shape=shape((len(blocks),) + blocks[0].shape),
        in_specs=[ANY] * (len(blocks) + len(deps)),
        out_specs=ANY,
        scratch_shapes=[pltpu.SemaphoreType.DMA((len(blocks),))],
        compiler_params=params(1 << 20),
        cost_estimate=cost(0, 4 * len(blocks) * blocks[0].size),
    )(*blocks, *deps)


def gather_rows(me, i, parts, rows):
    at = 0
    for part in parts:
        _, n_dp, count, width = part.shape
        for k in range(n_dp):
            cols = pl.ds(pl.multiple_of((me[0] ^ k) * width, 128), width)
            rows[at : at + count, cols] = part[i, k]
        at += count


class Stream:
    def __init__(self, copies):
        self.copies = copies
        self.started = 0

    def start(self, upto):
        while self.started < min(upto, len(self.copies)):
            for copy in self.copies[self.started]:
                copy.start()
            self.started += 1

    def take(self, i):
        for copy in self.copies[i]:
            copy.wait()


def slab_kernel(count, me, *refs):
    parts, (gw, uw, dw, out, rows, gate, up, wide, tall, wide_sem, tall_sem) = refs[:count], refs[count:]
    ff, piece = gw.shape[1], tall.shape[1]
    _, n_dp, _, width = parts[0].shape
    sub = wide.shape[2]
    forth = []
    for k in range(n_dp):
        for s in range(width // sub):
            source = pl.ds(pl.multiple_of((me[0] ^ k) * width + s * sub, 128), sub)
            slot = len(forth) % 3
            forth.append([
                pltpu.make_async_copy(w.at[source], wide.at[slot, j], wide_sem.at[slot, j])
                for j, w in enumerate((gw, uw))
            ])
    back = Stream([
        [pltpu.make_async_copy(dw.at[pl.ds(i * piece, piece)], tall.at[i % 3], tall_sem.at[i % 3])]
        for i in range(ff // piece)
    ])
    forth = Stream(forth)
    forth.start(2)
    total = len(forth.copies)
    for i in range(total):
        k, s = i // (width // sub), i % (width // sub)
        forth.take(i)
        forth.start(i + 3)
        if i >= total - 2:
            back.start(i + 3 - total)
        some = jnp.concatenate([p[0, k, :, s * sub : (s + 1) * sub] for p in parts])
        for acc, j in ((gate, 0), (up, 1)):
            more = mm(some, wide[i % 3, j])
            acc[...] = more if i == 0 else acc[...] + more
    gather_rows(me, 1, parts, rows)
    g, u = gate[...], up[...]
    sig = jax.nn.sigmoid(g)
    act = g * sig
    gate[...] = act
    out[:, :ff] = (act * u).astype(BF16)
    up[...] = u * sig * (1.0 + g * (1.0 - sig))
    for i in range(ff // piece):
        at = i * piece
        cols = slice(at, at + piece)
        back.take(i)
        back.start(i + 3)
        grad = mm(rows[...], tall[i % 3], LAST)
        out[:, ff + at : ff + at + piece] = (grad * up[:, cols]).astype(BF16)
        out[:, 2 * ff + at : 2 * ff + at + piece] = (grad * gate[:, cols]).astype(BF16)


def slab(me, parts, gw, uw, dw):
    rows, (d, ff) = sum(p.shape[2] for p in parts), gw.shape
    width = parts[0].shape[3]
    sub = 768 if width % 768 == 0 else width
    return pl.pallas_call(
        functools.partial(slab_kernel, len(parts)),
        out_shape=shape((rows, 3 * ff)),
        in_specs=[SMEM] + [VMEM] * len(parts) + [ANY] * 3,
        out_specs=VMEM,
        scratch_shapes=[
            pltpu.VMEM((rows, d), BF16),
            pltpu.VMEM((rows, ff), F32),
            pltpu.VMEM((rows, ff), F32),
            pltpu.VMEM((3, 2, sub, ff), BF16),
            pltpu.VMEM((3, 256, d), BF16),
            pltpu.SemaphoreType.DMA((3, 2)),
            pltpu.SemaphoreType.DMA((3,)),
        ],
        compiler_params=params(50 << 20),
        cost_estimate=cost(6 * rows * gw.size, 6 * gw.size, 1),
    )(me, *parts, gw, uw, dw)


def term_kernel(grads, gw, uw, *refs):
    mine, left, right, held, sem = refs[-5:]
    ff, half, width = gw.shape[1], mine.shape[0], mine.shape[1]
    tile = held.shape[2]
    copies = []
    for i in range(width // tile):
        rows, slot = pl.ds(i * tile, tile), i % 4
        copies.append([
            pltpu.make_async_copy(w.at[rows], held.at[slot, j], sem.at[slot, j]) for j, w in enumerate((gw, uw))
        ])
    stream = Stream(copies)
    stream.start(3)
    for i in range(width // tile):
        cols = slice(i * tile, (i + 1) * tile)
        stream.take(i)
        stream.start(i + 4)
        held_gate, held_up = held[i % 4, 0], held[i % 4, 1]
        term = mm(grads[:, ff : 2 * ff], held_gate, LAST) + mm(grads[:, 2 * ff :], held_up, LAST)
        mine[:, cols] = term[:half].astype(BF16)
        theirs = left if i * tile < width // 2 else right
        theirs[:, i * tile % (width // 2) : i * tile % (width // 2) + tile] = term[half:].astype(BF16)


def term(grads, gw, uw, deps):
    rows, (d, ff) = grads.shape[0], gw.shape
    return pl.pallas_call(
        term_kernel,
        out_shape=(shape((rows // 2, d)), shape((rows // 2, d // 2)), shape((rows // 2, d // 2))),
        in_specs=[VMEM, ANY, ANY] + [ANY] * len(deps),
        out_specs=(VMEM,) * 3,
        scratch_shapes=[pltpu.VMEM((4, 2, 512, ff), BF16), pltpu.SemaphoreType.DMA((4, 2))],
        compiler_params=params(50 << 20),
        cost_estimate=cost(4 * rows * gw.size, 4 * gw.size),
    )(grads, gw, uw, *deps)


def fold_kernel(mine, left, right, *outs):
    half = left.shape[1]
    for i, out in enumerate(outs):
        rows = slice(i * CAP, (i + 1) * CAP)
        for cols, theirs in ((slice(0, half), left), (slice(half, 2 * half), right)):
            out[:, cols] = (mine[rows, cols].astype(F32) + theirs[rows].astype(F32)).astype(BF16)


def fold(mine, left, right):
    rows, d = mine.shape
    return pl.pallas_call(
        fold_kernel,
        out_shape=[shape((CAP, d))] * (rows // CAP),
        in_specs=[VMEM] * 3,
        out_specs=[VMEM] * (rows // CAP),
        compiler_params=params(16 << 20),
        cost_estimate=cost(0, 6 * rows * d),
    )(mine, left, right)


def put_kernel(groups, sel, *refs):
    *parts, out = refs
    each = len(parts) // groups
    for g in range(groups):
        total = parts[g * each][...].astype(F32)
        for part in parts[g * each + 1 : (g + 1) * each]:
            total = total + part[...].astype(F32)
        width = total.shape[1]
        out[:, g * width : (g + 1) * width] = mm(sel[...], total.astype(BF16), ROWS).astype(BF16)


def put(sel, groups):
    parts = [p for group in groups for p in group]
    d = sum(group[0].shape[1] for group in groups)
    return pl.pallas_call(
        functools.partial(put_kernel, len(groups)),
        out_shape=shape((sel.shape[1], d)),
        in_specs=[VMEM] * (1 + len(parts)),
        out_specs=VMEM,
        compiler_params=params(32 << 20),
        cost_estimate=cost(2 * sel.size * d, 4 * sel.size * d),
    )(sel, *parts)


def contract_kernel(n_slices, n_grads, n_totals, *refs):
    slices, refs = refs[:n_slices], refs[n_slices:]
    grads, refs = refs[:n_grads], refs[n_grads:]
    totals, refs = refs[:n_totals], refs[n_totals:]
    outs, (picked, scaled, rows) = refs[:3], refs[3:]

    @pl.when(pl.program_id(0) == 0)
    def _():
        at = 0
        for block in slices:
            size = block.shape[-2]
            whole = len(block.shape) == 4
            picked[at : at + size] = block[0, 0] if whole else block[0]
            scaled[at : at + size] = block[1, 0] if whole else block[1]
            at += size
        at = 0
        for block in grads:
            size = block.shape[0]
            rows[at : at + size] = block[...]
            at += size

    ff, tile = rows.shape[1] // 3, outs[0].shape[0]
    cols = pl.ds(pl.multiple_of(pl.program_id(0) * tile, tile), tile)

    def put_tile(n, value):
        if n_totals:
            value = value + totals[n][...].astype(F32)
        outs[n][...] = value.astype(outs[n].dtype)

    put_tile(0, mm(picked[:, cols], rows[:, ff : 2 * ff], ROWS))
    put_tile(1, mm(picked[:, cols], rows[:, 2 * ff :], ROWS))
    put_tile(2, mm(rows[:, :ff], scaled[:, cols], ROWS))


def contract(slices, grads, totals, tile=256):
    rows = sum(b.shape[0] for b in grads)
    width, ff = slices[0].shape[-1], grads[0].shape[1] // 3
    tall = pl.BlockSpec((tile, ff), lambda i: (i, 0))
    wide = pl.BlockSpec((ff, tile), lambda i: (0, i))
    return pl.pallas_call(
        functools.partial(contract_kernel, len(slices), len(grads), len(totals)),
        out_shape=(shape((width, ff)), shape((width, ff)), shape((ff, width))),
        grid=(width // tile,),
        in_specs=[VMEM] * (len(slices) + len(grads)) + [tall, tall, wide][: len(totals)],
        out_specs=(tall, tall, wide),
        scratch_shapes=[pltpu.VMEM((rows, width), BF16)] * 2 + [pltpu.VMEM((rows, 3 * ff), BF16)],
        compiler_params=params(56 << 20),
        cost_estimate=cost(6 * rows * width * ff, 2 * rows * (2 * width + 3 * ff) + 12 * width * ff, 1),
    )(*slices, *grads, *totals)


def on_device(tokens, routes, route_probs, gate_weight, up_weight, down_weight, out_grad):
    n_dp, n_fetch = lax.axis_size("dp"), lax.axis_size("fetch")
    chips = n_fetch // 2
    me = lax.axis_index("dp").astype(jnp.int32).reshape(1)

    def move(x, hop):
        pairs = [(2 * z + c, 2 * ((z + hop) % chips) + c) for z in range(chips) for c in range(2)]
        return lax.ppermute(x, "fetch", pairs)

    def swap(x):
        return lax.ppermute(x, "fetch", [(k, k ^ 1) for k in range(n_fetch)])

    def across(x, bits):
        return lax.ppermute(x, "dp", [(k, k ^ bits) for k in range(n_dp)])

    offsets = [0]
    for s in range(1, chips // 2 + 1):
        offsets += [-s] if 2 * s == chips else [-s, s]

    sel, both = pick(me, tokens, routes, route_probs, out_grad, n_dp)
    blocks = {0: both, -1: move(both, 1)}
    blocks[0] = own = after(both, blocks[-1])
    for s in range(2, chips // 2 + 1):
        blocks[-s] = move(blocks[1 - s], 1)
    for s in range(1, chips // 2):
        blocks[s] = move(blocks[s - 1], -1)
    here, beside = [own, blocks[-1]], [blocks[o] for o in offsets[2:]]
    here_theirs = [swap(own), swap(blocks[-1])]
    near_cuts = lay(here, False, here_theirs[:1])
    near_got = [across(cut, k) for k, cut in enumerate(near_cuts, 1)]
    far, *far_cuts = lay(beside, True, near_got + here_theirs[1:])
    far_theirs = swap(far)
    far_got = [across(cut, k) for k, cut in enumerate(far_cuts, 1)]

    parts = here + [far] + here_theirs + [far_theirs]
    rows = slab(me, parts, gate_weight, up_weight, down_weight)
    mine, left, right = term(rows, gate_weight, up_weight, far_got)
    near_theirs = swap(pile(near_got, mine))
    far_got_theirs = swap(pile(far_got, mine))
    summed, *others = fold(mine, swap(left), swap(right))
    slices = [parts]
    for k in range(n_dp - 1):
        slices.append([near_got[k], far_got[k], near_theirs[k], far_got_theirs[k]])
    if n_dp == 4:
        half = rows.shape[0] // 2
        by_x, by_y = after(across(rows, 1), summed), after(across(rows, 2), summed)
        first = [rows, by_x, by_y]
        last = [across(by_x[:half], 2), across(by_y[half:], 1)]
    else:
        got = [across(rows, k) for k in range(1, n_dp)]
        first, last = [rows] + got[:-1], got[-1:]
    totals = contract(sum(slices[:-1], []), first, [])
    gate_grad, up_grad, down_grad = contract(slices[-1], last, totals)
    token_grad = put(sel, [[summed] + [move(x, o) for x, o in zip(others, offsets[1:])]])
    return token_grad, gate_grad, up_grad, down_grad


def solution(mesh):
    return jax.shard_map(
        on_device,
        mesh=mesh,
        in_specs=(
            P(("dp", "fetch"), None),
            P(("dp", "fetch"), None),
            P(("dp", "fetch"), None),
            P(None, "fetch"),
            P(None, "fetch"),
            P("fetch", None),
            P(("dp", "fetch"), None),
        ),
        out_specs=(P(("dp", "fetch"), None), P("dp", "fetch"), P("dp", "fetch"), P("fetch", "dp")),
        check_vma=False,
    )
```

```python
import functools

import jax
import jax.numpy as jnp
from jax import lax
from jax.experimental import pallas as pl
from jax.experimental.pallas import tpu as pltpu
from jax.sharding import PartitionSpec as P

CAP = 32
F32, BF16 = jnp.float32, jnp.bfloat16
ROWS = (((0,), (0,)), ((), ()))
LAST = (((1,), (1,)), ((), ()))
VMEM = pl.BlockSpec(memory_space=pltpu.VMEM)
SMEM = pl.BlockSpec(memory_space=pltpu.SMEM)
ANY = pl.BlockSpec(memory_space=pl.ANY)
LIMIT = 40 << 20


def mm(a, b, dims=(((1,), (0,)), ((), ()))):
    return lax.dot_general(a, b, dims, preferred_element_type=F32)


def shape(dims, kind=BF16):
    return jax.ShapeDtypeStruct(tuple(dims), kind)


def params(limit=LIMIT):
    return pltpu.CompilerParams(vmem_limit_bytes=limit)


def cost(flops, nbytes, weigh=64):
    return pl.CostEstimate(flops=int(flops) // weigh, bytes_accessed=int(nbytes) // weigh, transcendentals=0)


def fetch(source, held, sem, parts):
    width = source.shape[1] // parts
    copies = []
    for i in range(parts):
        cols = pl.ds(i * width, width)
        copies.append(pltpu.make_async_copy(source.at[:, cols], held.at[:, cols], sem.at[i]))
        copies[-1].start()
    return copies


def pick_kernel(me, routes, probs, tokens, out_grad, sel_out, both, again, held, sem):
    _, n_dp, _, width = both.shape
    copies = fetch(tokens, held.at[0], sem.at[0], n_dp) + fetch(out_grad, held.at[1], sem.at[1], n_dp)
    n = tokens.shape[0]
    hits = routes[...] == 0
    coef = jnp.sum(jnp.where(hits, probs[...], 0.0), axis=0, keepdims=True)
    routed = jnp.sum(jnp.where(hits, 1.0, 0.0), axis=0, keepdims=True) > 0.5
    flags = jnp.broadcast_to(jnp.where(routed, 1.0, 0.0), (8, n))
    before = lax.broadcasted_iota(jnp.int32, (n, n), 0) <= lax.broadcasted_iota(jnp.int32, (n, n), 1)
    upto = mm(flags.astype(BF16), jnp.where(before, 1.0, 0.0).astype(BF16))[:1]
    count = jnp.sum(flags[:1], axis=1, keepdims=True)
    lane = lax.broadcasted_iota(jnp.int32, (1, n), 1).astype(F32)
    rank = jnp.where(routed, upto - 1.0, count + lane - upto)
    sel = rank == lax.broadcasted_iota(jnp.int32, (CAP, n), 0).astype(F32)
    scale = jnp.sum(jnp.where(sel, coef, 0.0), axis=1, keepdims=True)
    sel = jnp.where(sel, 1.0, 0.0).astype(BF16)
    sel_out[...] = sel
    for copy in copies:
        copy.wait()
    for k in range(n_dp):
        cols = pl.ds(pl.multiple_of((me[0] ^ k) * width, 128), width)
        both[0, k] = mm(sel, held[0, :, cols]).astype(BF16)
        both[1, k] = (scale * mm(sel, held[1, :, cols])).astype(BF16)
        again[:, k] = both[:, k]


def pick(me, tokens, routes, probs, out_grad, n_dp):
    n, d = tokens.shape
    return pl.pallas_call(
        pick_kernel,
        out_shape=(shape((CAP, n)),) + (shape((2, n_dp, CAP, d // n_dp)),) * 2,
        in_specs=[SMEM, VMEM, VMEM, ANY, ANY],
        out_specs=(VMEM,) * 3,
        scratch_shapes=[pltpu.VMEM((2, n, d), BF16), pltpu.SemaphoreType.DMA((2, n_dp))],
        compiler_params=params(60 << 20),
        cost_estimate=cost(4 * CAP * n * d, 5 * n * d),
    )(me, routes.T, probs.T, tokens, out_grad)


def after(x, *deps):
    def kernel(*refs):
        del refs

    return pl.pallas_call(
        kernel,
        out_shape=shape(x.shape, x.dtype),
        in_specs=[ANY] * (1 + len(deps)),
        out_specs=ANY,
        input_output_aliases={0: 0},
        compiler_params=params(1 << 20),
        cost_estimate=cost(0, 0),
    )(x, *deps)


def lay_kernel(count, deps, whole, *refs):
    blocks, rest, sem = refs[:count], list(refs[count + deps : -1]), refs[-1]
    copies = []
    at = 0
    for b in blocks:
        rows = pl.ds(at, b.shape[2])
        at += b.shape[2]
        if whole:
            copies.append((b, rest[0].at[:, :, rows]))
        for k, out in enumerate(rest[whole:], 1):
            copies.append((b.at[:, k], out.at[:, rows]))
    copies = [pltpu.make_async_copy(a, b, sem.at[i]) for i, (a, b) in enumerate(copies)]
    for copy in copies:
        copy.start()
    for copy in copies:
        copy.wait()


def lay(blocks, whole, deps=()):
    arrays, slices, _, width = blocks[0].shape
    rows = sum(b.shape[2] for b in blocks)
    cut = slices - 1
    outs = [shape((arrays, slices, rows, width))] * whole + [shape((arrays, rows, width))] * cut
    return pl.pallas_call(
        functools.partial(lay_kernel, len(blocks), len(deps), whole),
        out_shape=outs,
        in_specs=[ANY] * (len(blocks) + len(deps)),
        out_specs=[ANY] * len(outs),
        scratch_shapes=[pltpu.SemaphoreType.DMA((len(blocks) * (whole + cut),))],
        compiler_params=params(1 << 20),
        cost_estimate=cost(0, 4 * arrays * slices * rows * width),
    )(*blocks, *deps)


def pile_kernel(count, *refs):
    blocks, out, sem = refs[:count], refs[-2], refs[-1]
    copies = [pltpu.make_async_copy(b, out.at[i], sem.at[i]) for i, b in enumerate(blocks)]
    for copy in copies:
        copy.start()
    for copy in copies:
        copy.wait()


def pile(blocks, *deps):
    return pl.pallas_call(
        functools.partial(pile_kernel, len(blocks)),
        out_shape=shape((len(blocks),) + blocks[0].shape),
        in_specs=[ANY] * (len(blocks) + len(deps)),
        out_specs=ANY,
        scratch_shapes=[pltpu.SemaphoreType.DMA((len(blocks),))],
        compiler_params=params(1 << 20),
        cost_estimate=cost(0, 4 * len(blocks) * blocks[0].size),
    )(*blocks, *deps)


def gather_rows(me, i, parts, rows):
    at = 0
    for part in parts:
        _, n_dp, count, width = part.shape
        for k in range(n_dp):
            cols = pl.ds(pl.multiple_of((me[0] ^ k) * width, 128), width)
            rows[at : at + count, cols] = part[i, k]
        at += count


class Stream:
    def __init__(self, copies):
        self.copies = copies
        self.started = 0

    def start(self, upto):
        while self.started < min(upto, len(self.copies)):
            for copy in self.copies[self.started]:
                copy.start()
            self.started += 1

    def take(self, i):
        for copy in self.copies[i]:
            copy.wait()


def slab_kernel(count, sides, me, *refs):
    parts, refs = refs[:count], refs[count:]
    gw, uw, dw, out, mine, left, right, rows, gate, up, wide, tall, wide_sem, tall_sem = refs
    ff, piece = gw.shape[1], tall.shape[1]
    _, n_dp, _, width = parts[0].shape
    sub = 768 if width % 768 == 0 else width
    steps = width // sub
    forth, spans = [], []
    for k in range(n_dp):
        for s in range(steps):
            span = pl.ds(pl.multiple_of((me[0] ^ k) * width + s * sub, 128), sub)
            slot = len(forth) % 4
            spans.append(span)
            forth.append([
                pltpu.make_async_copy(w.at[span], wide.at[j, span], wide_sem.at[slot, j]) for j, w in enumerate((gw, uw))
            ])
    back = Stream([
        [pltpu.make_async_copy(dw.at[pl.ds(i * piece, piece)], tall.at[i % 3], tall_sem.at[i % 3])]
        for i in range(ff // piece)
    ])
    forth = Stream(forth)
    forth.start(1)
    gather_rows(me, 1, parts, rows)
    forth.start(3)
    for i, span in enumerate(spans):
        k, s = i // steps, i % steps
        forth.take(i)
        forth.start(i + 4)
        if i >= len(spans) - 2:
            back.start(i + 3 - len(spans))
        some = jnp.concatenate([p[0, k, :, s * sub : (s + 1) * sub] for p in parts])
        for acc, j in ((gate, 0), (up, 1)):
            more = mm(some, wide[j, span])
            acc[...] = more if i == 0 else acc[...] + more
    g, u = gate[...], up[...]
    sig = jax.nn.sigmoid(g)
    act = g * sig
    gate[...] = act
    out[:, :ff] = (act * u).astype(BF16)
    up[...] = u * sig * (1.0 + g * (1.0 - sig))
    for i in range(ff // piece):
        at = i * piece
        cols = slice(at, at + piece)
        back.take(i)
        back.start(i + 3)
        grad = mm(rows[...], tall[i % 3], LAST)
        out[:, ff + at : ff + at + piece] = (grad * up[:, cols]).astype(BF16)
        out[:, 2 * ff + at : 2 * ff + at + piece] = (grad * gate[:, cols]).astype(BF16)
    d = wide.shape[1]
    tile = 512
    for i in range(d // tile):
        cols = slice(i * tile, (i + 1) * tile)
        half = slice(i * tile % (d // 2), i * tile % (d // 2) + tile)
        theirs = left if i * tile < d // 2 else right
        term = mm(out[:, ff : 2 * ff], wide[0, cols], LAST) + mm(out[:, 2 * ff :], wide[1, cols], LAST)
        at, to = 0, [0, 0]
        for side, size in sides:
            some = term[at : at + size].astype(BF16)
            if side == 0:
                mine[to[0] : to[0] + size, cols] = some
            else:
                theirs[to[1] : to[1] + size, half] = some
            at += size
            to[side] += size


def slab(me, parts, sides, gw, uw, dw, dep):
    sizes = [p.shape[2] for p in parts]
    rows, (d, ff) = sum(sizes), gw.shape
    n = len(parts) + 3

    def kernel(me, *refs):
        slab_kernel(len(parts), tuple(zip(sides, sizes)), me, *refs[:n], *refs[n + 1 :])

    return pl.pallas_call(
        kernel,
        out_shape=(
            shape((rows, 3 * ff)),
            shape((rows // 2, d)),
            shape((rows // 2, d // 2)),
            shape((rows // 2, d // 2)),
        ),
        in_specs=[SMEM] + [VMEM] * len(parts) + [ANY] * 4,
        out_specs=(VMEM,) * 4,
        scratch_shapes=[
            pltpu.VMEM((rows, d), BF16),
            pltpu.VMEM((rows, ff), F32),
            pltpu.VMEM((rows, ff), F32),
            pltpu.VMEM((2, d, ff), BF16),
            pltpu.VMEM((3, 256, d), BF16),
            pltpu.SemaphoreType.DMA((4, 2)),
            pltpu.SemaphoreType.DMA((3,)),
        ],
        compiler_params=params(46 << 20),
        cost_estimate=cost(10 * rows * gw.size, 6 * gw.size, 1),
    )(me, *parts, gw, uw, dw, dep)


def fold_kernel(mine, left, right, _, *outs):
    half = left.shape[1]
    for i, out in enumerate(outs):
        rows = slice(i * CAP, (i + 1) * CAP)
        for cols, theirs in ((slice(0, half), left), (slice(half, 2 * half), right)):
            out[:, cols] = (mine[rows, cols].astype(F32) + theirs[rows].astype(F32)).astype(BF16)


def fold(mine, left, right, dep):
    rows, d = mine.shape
    return pl.pallas_call(
        fold_kernel,
        out_shape=[shape((CAP, d))] * (rows // CAP),
        in_specs=[VMEM] * 3 + [ANY],
        out_specs=[VMEM] * (rows // CAP),
        compiler_params=params(16 << 20),
        cost_estimate=cost(0, 6 * rows * d),
    )(mine, left, right, dep)


def put_kernel(groups, sel, _, *refs):
    *parts, out = refs
    each = len(parts) // groups
    for g in range(groups):
        total = parts[g * each][...].astype(F32)
        for part in parts[g * each + 1 : (g + 1) * each]:
            total = total + part[...].astype(F32)
        width = total.shape[1]
        out[:, g * width : (g + 1) * width] = mm(sel[...], total.astype(BF16), ROWS).astype(BF16)


def put(sel, groups, dep):
    parts = [p for group in groups for p in group]
    d = sum(group[0].shape[1] for group in groups)
    return pl.pallas_call(
        functools.partial(put_kernel, len(groups)),
        out_shape=shape((sel.shape[1], d)),
        in_specs=[VMEM, ANY] + [VMEM] * len(parts),
        out_specs=VMEM,
        compiler_params=params(32 << 20),
        cost_estimate=cost(2 * sel.size * d, 4 * sel.size * d),
    )(sel, dep, *parts)


def contract_kernel(n_slices, n_grads, n_totals, *refs):
    slices, refs = refs[:n_slices], refs[n_slices:]
    grads, refs = refs[:n_grads], refs[n_grads:]
    totals, refs = refs[:n_totals], refs[n_totals:]
    outs, (picked, scaled, rows) = refs[:3], refs[3:]

    @pl.when(pl.program_id(0) == 0)
    def _():
        at = 0
        for block in slices:
            size = block.shape[-2]
            whole = len(block.shape) == 4
            picked[at : at + size] = block[0, 0] if whole else block[0]
            scaled[at : at + size] = block[1, 0] if whole else block[1]
            at += size
        at = 0
        for block in grads:
            size = block.shape[0]
            rows[at : at + size] = block[...]
            at += size

    ff, tile = rows.shape[1] // 3, outs[0].shape[0]
    cols = pl.ds(pl.multiple_of(pl.program_id(0) * tile, tile), tile)

    def put_tile(n, value):
        if n_totals:
            value = value + totals[n][...].astype(F32)
        outs[n][...] = value.astype(outs[n].dtype)

    put_tile(0, mm(picked[:, cols], rows[:, ff : 2 * ff], ROWS))
    put_tile(1, mm(picked[:, cols], rows[:, 2 * ff :], ROWS))
    put_tile(2, mm(rows[:, :ff], scaled[:, cols], ROWS))


def contract(slices, grads, totals, tile=512):
    rows = sum(b.shape[0] for b in grads)
    width, ff = slices[0].shape[-1], grads[0].shape[1] // 3
    tile = tile if width % tile == 0 else 256
    tall = pl.BlockSpec((tile, ff), lambda i: (i, 0))
    wide = pl.BlockSpec((ff, tile), lambda i: (0, i))
    return pl.pallas_call(
        functools.partial(contract_kernel, len(slices), len(grads), len(totals)),
        out_shape=(shape((width, ff)), shape((width, ff)), shape((ff, width))),
        grid=(width // tile,),
        in_specs=[VMEM] * (len(slices) + len(grads)) + [tall, tall, wide][: len(totals)],
        out_specs=(tall, tall, wide),
        scratch_shapes=[pltpu.VMEM((rows, width), BF16)] * 2 + [pltpu.VMEM((rows, 3 * ff), BF16)],
        compiler_params=params(56 << 20),
        cost_estimate=cost(6 * rows * width * ff, 2 * rows * (2 * width + 3 * ff) + 12 * width * ff, 1),
    )(*slices, *grads, *totals)


def on_device(tokens, routes, route_probs, gate_weight, up_weight, down_weight, out_grad):
    n_dp, n_fetch = lax.axis_size("dp"), lax.axis_size("fetch")
    chips = n_fetch // 2
    me = lax.axis_index("dp").astype(jnp.int32).reshape(1)

    def move(x, hop):
        pairs = [(2 * z + c, 2 * ((z + hop) % chips) + c) for z in range(chips) for c in range(2)]
        return lax.ppermute(x, "fetch", pairs)

    def swap(x):
        return lax.ppermute(x, "fetch", [(k, k ^ 1) for k in range(n_fetch)])

    def across(x, bits):
        return lax.ppermute(x, "dp", [(k, k ^ bits) for k in range(n_dp)])

    offsets = [0]
    for s in range(1, chips // 2 + 1):
        offsets += [-s] if 2 * s == chips else [-s, s]

    sel, own, again = pick(me, tokens, routes, route_probs, out_grad, n_dp)
    blocks = {0: own, -1: move(own, 1)}
    for s in range(2, chips // 2 + 1):
        blocks[-s] = move(blocks[1 - s], 1)
    for s in range(1, chips // 2):
        blocks[s] = move(after(again, blocks[-1]) if s == 1 else blocks[s - 1], -1)
    here, beside = [own, blocks[-1]], [blocks[o] for o in offsets[2:]]
    here_theirs = [swap(x) for x in here]
    near_cuts = lay(here, False, here_theirs[:1])
    near_got = [across(cut, k) for k, cut in enumerate(near_cuts, 1)]
    far, *far_cuts = lay(beside, True, near_got + here_theirs[1:])
    far_theirs = swap(far)
    far_got = [across(cut, k) for k, cut in enumerate(far_cuts, 1)]
    near_theirs = swap(pile(near_got))

    parts = here + [far] + here_theirs + [far_theirs]
    rows, mine, left, right = slab(me, parts, (0, 0, 0, 1, 1, 1), gate_weight, up_weight, down_weight, near_theirs)
    far_got_theirs = swap(pile(far_got, left))
    summed, *others = fold(mine, swap(after(left, *far_got)), swap(right), far_got_theirs)
    slices = [parts]
    for k in range(n_dp - 1):
        slices.append([near_got[k], far_got[k], near_theirs[k], far_got_theirs[k]])
    if n_dp == 4:
        half = rows.shape[0] // 2
        by_x, by_y = after(across(rows, 1), summed), after(across(rows, 2), summed)
        first = [rows, by_x, by_y]
        last = [across(by_x[:half], 2), across(by_y[half:], 1)]
    else:
        got = [across(rows, k) for k in range(1, n_dp)]
        first, last = [rows] + got[:-1], got[-1:]
    totals = contract(sum(slices[:-1], []), first, [])
    gate_grad, up_grad, down_grad = contract(slices[-1], last, totals)
    token_grad = put(sel, [[summed] + [move(x, o) for x, o in zip(others, offsets[1:])]], totals[2])
    return token_grad, gate_grad, up_grad, down_grad


def solution(mesh):
    return jax.shard_map(
        on_device,
        mesh=mesh,
        in_specs=(
            P(("dp", "fetch"), None),
            P(("dp", "fetch"), None),
            P(("dp", "fetch"), None),
            P(None, "fetch"),
            P(None, "fetch"),
            P("fetch", None),
            P(("dp", "fetch"), None),
        ),
        out_specs=(P(("dp", "fetch"), None), P("dp", "fetch"), P("dp", "fetch"), P("fetch", "dp")),
        check_vma=False,
    )
```

```python
import functools

import jax
import jax.numpy as jnp
from jax import lax
from jax.experimental import pallas as pl
from jax.experimental.pallas import tpu as pltpu
from jax.sharding import PartitionSpec as P

CAP = 32
F32, BF16 = jnp.float32, jnp.bfloat16
ROWS = (((0,), (0,)), ((), ()))
LAST = (((1,), (1,)), ((), ()))
VMEM = pl.BlockSpec(memory_space=pltpu.VMEM)
SMEM = pl.BlockSpec(memory_space=pltpu.SMEM)
ANY = pl.BlockSpec(memory_space=pl.ANY)
LIMIT = 40 << 20


def mm(a, b, dims=(((1,), (0,)), ((), ()))):
    return lax.dot_general(a, b, dims, preferred_element_type=F32)


def shape(dims, kind=BF16):
    return jax.ShapeDtypeStruct(tuple(dims), kind)


def params(limit=LIMIT):
    return pltpu.CompilerParams(vmem_limit_bytes=limit)


def cost(flops, nbytes, weigh=64):
    return pl.CostEstimate(flops=int(flops) // weigh, bytes_accessed=int(nbytes) // weigh, transcendentals=0)


def fetch(source, held, sem, parts):
    width = source.shape[1] // parts
    copies = []
    for i in range(parts):
        cols = pl.ds(i * width, width)
        copies.append(pltpu.make_async_copy(source.at[:, cols], held.at[:, cols], sem.at[i]))
        copies[-1].start()
    return copies


def pick_kernel(me, routes, probs, tokens, out_grad, sel_out, both, again, held, sem):
    _, n_dp, _, width = both.shape
    copies = fetch(tokens, held.at[0], sem.at[0], n_dp) + fetch(out_grad, held.at[1], sem.at[1], n_dp)
    n = tokens.shape[0]
    hits = routes[...] == 0
    coef = jnp.sum(jnp.where(hits, probs[...], 0.0), axis=0, keepdims=True)
    routed = jnp.sum(jnp.where(hits, 1.0, 0.0), axis=0, keepdims=True) > 0.5
    flags = jnp.broadcast_to(jnp.where(routed, 1.0, 0.0), (8, n))
    before = lax.broadcasted_iota(jnp.int32, (n, n), 0) <= lax.broadcasted_iota(jnp.int32, (n, n), 1)
    upto = mm(flags.astype(BF16), jnp.where(before, 1.0, 0.0).astype(BF16))[:1]
    count = jnp.sum(flags[:1], axis=1, keepdims=True)
    lane = lax.broadcasted_iota(jnp.int32, (1, n), 1).astype(F32)
    rank = jnp.where(routed, upto - 1.0, count + lane - upto)
    sel = rank == lax.broadcasted_iota(jnp.int32, (CAP, n), 0).astype(F32)
    scale = jnp.sum(jnp.where(sel, coef, 0.0), axis=1, keepdims=True)
    sel = jnp.where(sel, 1.0, 0.0).astype(BF16)
    sel_out[...] = sel
    for copy in copies:
        copy.wait()
    for k in range(n_dp):
        cols = pl.ds(pl.multiple_of((me[0] ^ k) * width, 128), width)
        both[0, k] = mm(sel, held[0, :, cols]).astype(BF16)
        both[1, k] = (scale * mm(sel, held[1, :, cols])).astype(BF16)
        again[:, k] = both[:, k]


def pick(me, tokens, routes, probs, out_grad, n_dp):
    n, d = tokens.shape
    return pl.pallas_call(
        pick_kernel,
        out_shape=(shape((CAP, n)),) + (shape((2, n_dp, CAP, d // n_dp)),) * 2,
        in_specs=[SMEM, VMEM, VMEM, ANY, ANY],
        out_specs=(VMEM,) * 3,
        scratch_shapes=[pltpu.VMEM((2, n, d), BF16), pltpu.SemaphoreType.DMA((2, n_dp))],
        compiler_params=params(60 << 20),
        cost_estimate=cost(4 * CAP * n * d, 5 * n * d),
    )(me, routes.T, probs.T, tokens, out_grad)


def after(x, *deps):
    def kernel(*refs):
        del refs

    return pl.pallas_call(
        kernel,
        out_shape=shape(x.shape, x.dtype),
        in_specs=[ANY] * (1 + len(deps)),
        out_specs=ANY,
        input_output_aliases={0: 0},
        compiler_params=params(1 << 20),
        cost_estimate=cost(0, 0),
    )(x, *deps)


def lay_kernel(count, deps, whole, *refs):
    blocks, rest, sem = refs[:count], list(refs[count + deps : -1]), refs[-1]
    copies = []
    at = 0
    for b in blocks:
        rows = pl.ds(at, b.shape[2])
        at += b.shape[2]
        if whole:
            copies.append((b, rest[0].at[:, :, rows]))
        for k, out in enumerate(rest[whole:], 1):
            copies.append((b.at[:, k], out.at[:, rows]))
    copies = [pltpu.make_async_copy(a, b, sem.at[i]) for i, (a, b) in enumerate(copies)]
    for copy in copies:
        copy.start()
    for copy in copies:
        copy.wait()


def lay(blocks, whole, deps=()):
    arrays, slices, _, width = blocks[0].shape
    rows = sum(b.shape[2] for b in blocks)
    cut = slices - 1
    outs = [shape((arrays, slices, rows, width))] * whole + [shape((arrays, rows, width))] * cut
    return pl.pallas_call(
        functools.partial(lay_kernel, len(blocks), len(deps), whole),
        out_shape=outs,
        in_specs=[ANY] * (len(blocks) + len(deps)),
        out_specs=[ANY] * len(outs),
        scratch_shapes=[pltpu.SemaphoreType.DMA((len(blocks) * (whole + cut),))],
        compiler_params=params(1 << 20),
        cost_estimate=cost(0, 4 * arrays * slices * rows * width),
    )(*blocks, *deps)


def pile_kernel(count, *refs):
    blocks, out, sem = refs[:count], refs[-2], refs[-1]
    copies = [pltpu.make_async_copy(b, out.at[i], sem.at[i]) for i, b in enumerate(blocks)]
    for copy in copies:
        copy.start()
    for copy in copies:
        copy.wait()


def pile(blocks, *deps):
    return pl.pallas_call(
        functools.partial(pile_kernel, len(blocks)),
        out_shape=shape((len(blocks),) + blocks[0].shape),
        in_specs=[ANY] * (len(blocks) + len(deps)),
        out_specs=ANY,
        scratch_shapes=[pltpu.SemaphoreType.DMA((len(blocks),))],
        compiler_params=params(1 << 20),
        cost_estimate=cost(0, 4 * len(blocks) * blocks[0].size),
    )(*blocks, *deps)


def gather_rows(me, i, parts, rows):
    at = 0
    for part in parts:
        _, n_dp, count, width = part.shape
        for k in range(n_dp):
            cols = pl.ds(pl.multiple_of((me[0] ^ k) * width, 128), width)
            rows[at : at + count, cols] = part[i, k]
        at += count


class Stream:
    def __init__(self, copies):
        self.copies = copies
        self.started = 0

    def start(self, upto):
        while self.started < min(upto, len(self.copies)):
            for copy in self.copies[self.started]:
                copy.start()
            self.started += 1

    def take(self, i):
        for copy in self.copies[i]:
            copy.wait()


def slab_kernel(count, sides, me, *refs):
    parts, refs = refs[:count], refs[count:]
    gw, uw, dw, out, mine, left, right, rows, gate, up, wide, tall, wide_sem, tall_sem = refs
    ff, piece = gw.shape[1], tall.shape[1]
    _, n_dp, _, width = parts[0].shape
    sub = 768 if width % 768 == 0 else width
    steps = width // sub
    forth, spans = [], []
    for k in range(n_dp):
        for s in range(steps):
            span = pl.ds(pl.multiple_of((me[0] ^ k) * width + s * sub, 128), sub)
            slot = len(forth) % 4
            spans.append(span)
            forth.append([
                pltpu.make_async_copy(w.at[span], wide.at[j, span], wide_sem.at[slot, j]) for j, w in enumerate((gw, uw))
            ])
    back = Stream([
        [pltpu.make_async_copy(dw.at[pl.ds(i * piece, piece)], tall.at[i % 2], tall_sem.at[i % 2])]
        for i in range(ff // piece)
    ])
    forth = Stream(forth)
    forth.start(1)
    gather_rows(me, 1, parts, rows)
    forth.start(3)
    for i, span in enumerate(spans):
        k, s = i // steps, i % steps
        forth.take(i)
        forth.start(i + 4)
        if i >= len(spans) - 2:
            back.start(i + 3 - len(spans))
        some = jnp.concatenate([p[0, k, :, s * sub : (s + 1) * sub] for p in parts])
        for acc, j in ((gate, 0), (up, 1)):
            more = mm(some, wide[j, span])
            acc[...] = more if i == 0 else acc[...] + more
    g, u = gate[...], up[...]
    sig = jax.nn.sigmoid(g)
    act = g * sig
    gate[...] = act
    out[:, :ff] = (act * u).astype(BF16)
    up[...] = u * sig * (1.0 + g * (1.0 - sig))
    for i in range(ff // piece):
        at = i * piece
        cols = slice(at, at + piece)
        back.take(i)
        grad = mm(rows[...], tall[i % 2], LAST)
        out[:, ff + at : ff + at + piece] = (grad * up[:, cols]).astype(BF16)
        out[:, 2 * ff + at : 2 * ff + at + piece] = (grad * gate[:, cols]).astype(BF16)
        back.start(i + 3)
    d = wide.shape[1]
    tile = 512
    for i in range(d // tile):
        cols = slice(i * tile, (i + 1) * tile)
        half = slice(i * tile % (d // 2), i * tile % (d // 2) + tile)
        theirs = left if i * tile < d // 2 else right
        term = mm(out[:, ff : 2 * ff], wide[0, cols], LAST) + mm(out[:, 2 * ff :], wide[1, cols], LAST)
        at, to = 0, [0, 0]
        for side, size in sides:
            some = term[at : at + size].astype(BF16)
            if side == 0:
                mine[to[0] : to[0] + size, cols] = some
            else:
                theirs[to[1] : to[1] + size, half] = some
            at += size
            to[side] += size


def slab(me, parts, sides, gw, uw, dw, dep):
    sizes = [p.shape[2] for p in parts]
    rows, (d, ff) = sum(sizes), gw.shape
    n = len(parts) + 3

    def kernel(me, *refs):
        slab_kernel(len(parts), tuple(zip(sides, sizes)), me, *refs[:n], *refs[n + 1 :])

    return pl.pallas_call(
        kernel,
        out_shape=(
            shape((rows, 3 * ff)),
            shape((rows // 2, d)),
            shape((rows // 2, d // 2)),
            shape((rows // 2, d // 2)),
        ),
        in_specs=[SMEM] + [VMEM] * len(parts) + [ANY] * 4,
        out_specs=(VMEM,) * 4,
        scratch_shapes=[
            pltpu.VMEM((rows, d), BF16),
            pltpu.VMEM((rows, ff), F32),
            pltpu.VMEM((rows, ff), F32),
            pltpu.VMEM((2, d, ff), BF16),
            pltpu.VMEM((2, 256, d), BF16),
            pltpu.SemaphoreType.DMA((4, 2)),
            pltpu.SemaphoreType.DMA((2,)),
        ],
        compiler_params=params(42 << 20),
        cost_estimate=cost(10 * rows * gw.size, 6 * gw.size, 1),
    )(me, *parts, gw, uw, dw, dep)


def fold_kernel(mine, left, right, _, *outs):
    half = left.shape[1]
    for i, out in enumerate(outs):
        rows = slice(i * CAP, (i + 1) * CAP)
        for cols, theirs in ((slice(0, half), left), (slice(half, 2 * half), right)):
            out[:, cols] = (mine[rows, cols].astype(F32) + theirs[rows].astype(F32)).astype(BF16)


def fold(mine, left, right, dep):
    rows, d = mine.shape
    return pl.pallas_call(
        fold_kernel,
        out_shape=[shape((CAP, d))] * (rows // CAP),
        in_specs=[VMEM] * 3 + [ANY],
        out_specs=[VMEM] * (rows // CAP),
        compiler_params=params(16 << 20),
        cost_estimate=cost(0, 6 * rows * d),
    )(mine, left, right, dep)


def put_kernel(groups, sel, _, *refs):
    *parts, out = refs
    each = len(parts) // groups
    for g in range(groups):
        total = parts[g * each][...].astype(F32)
        for part in parts[g * each + 1 : (g + 1) * each]:
            total = total + part[...].astype(F32)
        width = total.shape[1]
        out[:, g * width : (g + 1) * width] = mm(sel[...], total.astype(BF16), ROWS).astype(BF16)


def put(sel, groups, dep):
    parts = [p for group in groups for p in group]
    d = sum(group[0].shape[1] for group in groups)
    return pl.pallas_call(
        functools.partial(put_kernel, len(groups)),
        out_shape=shape((sel.shape[1], d)),
        in_specs=[VMEM, ANY] + [VMEM] * len(parts),
        out_specs=VMEM,
        compiler_params=params(32 << 20),
        cost_estimate=cost(2 * sel.size * d, 4 * sel.size * d),
    )(sel, dep, *parts)


def contract_kernel(n_slices, n_grads, n_totals, *refs):
    slices, refs = refs[:n_slices], refs[n_slices:]
    grads, refs = refs[:n_grads], refs[n_grads:]
    totals, refs = refs[:n_totals], refs[n_totals:]
    outs, mark, (picked, scaled, rows) = refs[:3], refs[3], refs[4:]
    mark[...] = jnp.zeros(mark.shape, F32)

    @pl.when(pl.program_id(0) == 0)
    def _():
        at = 0
        for block in slices:
            size = block.shape[-2]
            whole = len(block.shape) == 4
            picked[at : at + size] = block[0, 0] if whole else block[0]
            scaled[at : at + size] = block[1, 0] if whole else block[1]
            at += size
        at = 0
        for block in grads:
            size = block.shape[0]
            rows[at : at + size] = block[...]
            at += size

    ff, tile = rows.shape[1] // 3, outs[0].shape[0]
    cols = pl.ds(pl.multiple_of(pl.program_id(0) * tile, tile), tile)

    def put_tile(n, value):
        if n_totals:
            value = value + totals[n][...].astype(F32)
        outs[n][...] = value.astype(outs[n].dtype)

    put_tile(0, mm(picked[:, cols], rows[:, ff : 2 * ff], ROWS))
    put_tile(1, mm(picked[:, cols], rows[:, 2 * ff :], ROWS))
    put_tile(2, mm(rows[:, :ff], scaled[:, cols], ROWS))


def contract(slices, grads, totals, tile=512):
    rows = sum(b.shape[0] for b in grads)
    width, ff = slices[0].shape[-1], grads[0].shape[1] // 3
    tile = tile if width % tile == 0 else 256
    outs = (shape((width, ff)), shape((width, ff)), shape((ff, width)))
    held = 2 * rows * (2 * width + 3 * ff)
    tall = pl.BlockSpec((tile, ff), lambda i: (i, 0))
    wide = pl.BlockSpec((ff, tile), lambda i: (0, i))
    return pl.pallas_call(
        functools.partial(contract_kernel, len(slices), len(grads), len(totals)),
        out_shape=(list(outs) if totals else [pltpu.VMEM(o.shape, o.dtype) for o in outs]) + [shape((8, 128), F32)],
        grid=(width // tile,),
        in_specs=[VMEM] * (len(slices) + len(grads)) + [tall, tall, wide][: len(totals)],
        out_specs=[tall, tall, wide, pl.BlockSpec((8, 128), lambda i: (0, 0))],
        scratch_shapes=[pltpu.VMEM((rows, width), BF16)] * 2 + [pltpu.VMEM((rows, 3 * ff), BF16)],
        compiler_params=params((42 if held < 16 << 20 else 56) << 20),
        cost_estimate=cost(6 * rows * width * ff, 2 * rows * (2 * width + 3 * ff) + 12 * width * ff, 1),
    )(*slices, *grads, *totals)


def on_device(tokens, routes, route_probs, gate_weight, up_weight, down_weight, out_grad):
    n_dp, n_fetch = lax.axis_size("dp"), lax.axis_size("fetch")
    chips = n_fetch // 2
    me = lax.axis_index("dp").astype(jnp.int32).reshape(1)

    def move(x, hop):
        pairs = [(2 * z + c, 2 * ((z + hop) % chips) + c) for z in range(chips) for c in range(2)]
        return lax.ppermute(x, "fetch", pairs)

    def swap(x):
        return lax.ppermute(x, "fetch", [(k, k ^ 1) for k in range(n_fetch)])

    def across(x, bits):
        return lax.ppermute(x, "dp", [(k, k ^ bits) for k in range(n_dp)])

    offsets = [0]
    for s in range(1, chips // 2 + 1):
        offsets += [-s] if 2 * s == chips else [-s, s]

    sel, own, again = pick(me, tokens, routes, route_probs, out_grad, n_dp)
    blocks = {0: own, -1: move(own, 1)}
    for s in range(2, chips // 2 + 1):
        blocks[-s] = move(blocks[1 - s], 1)
    for s in range(1, chips // 2):
        blocks[s] = move(after(again, blocks[-1]) if s == 1 else blocks[s - 1], -1)
    here, beside = [own, blocks[-1]], [blocks[o] for o in offsets[2:]]
    here_theirs = [swap(x) for x in here]
    near_cuts = lay(here, False, here_theirs[:1])
    near_got = [across(cut, k) for k, cut in enumerate(near_cuts, 1)]
    far, *far_cuts = lay(beside, True, near_got + here_theirs[1:])
    far_theirs = swap(far)
    far_got = [across(cut, k) for k, cut in enumerate(far_cuts, 1)]
    near_theirs = swap(pile(near_got))

    parts = here + [far] + here_theirs + [far_theirs]
    rows, mine, left, right = slab(me, parts, (0, 0, 0, 1, 1, 1), gate_weight, up_weight, down_weight, near_theirs)
    far_got_theirs = swap(pile(far_got, left))
    summed, *others = fold(mine, swap(after(left, *far_got)), swap(right), far_got_theirs)
    slices = [parts]
    for k in range(n_dp - 1):
        slices.append([near_got[k], far_got[k], near_theirs[k], far_got_theirs[k]])
    if n_dp == 4:
        half = rows.shape[0] // 2
        by_x, by_y = after(across(rows, 1), summed), after(across(rows, 2), summed)
        first = [rows, by_x, by_y]
        last = [across(by_x[:half], 2), across(by_y[half:], 1)]
    else:
        got = [across(rows, k) for k in range(1, n_dp)]
        first, last = [rows] + got[:-1], got[-1:]
    *totals, mark = contract(sum(slices[:-1], []), first, [])
    gate_grad, up_grad, down_grad, _ = contract(slices[-1], last, totals)
    token_grad = put(sel, [[summed] + [move(x, o) for x, o in zip(others, offsets[1:])]], mark)
    return token_grad, gate_grad, up_grad, down_grad


def solution(mesh):
    return jax.shard_map(
        on_device,
        mesh=mesh,
        in_specs=(
            P(("dp", "fetch"), None),
            P(("dp", "fetch"), None),
            P(("dp", "fetch"), None),
            P(None, "fetch"),
            P(None, "fetch"),
            P("fetch", None),
            P(("dp", "fetch"), None),
        ),
        out_specs=(P(("dp", "fetch"), None), P("dp", "fetch"), P("dp", "fetch"), P("fetch", "dp")),
        check_vma=False,
    )
```

```python
import functools

import jax
import jax.numpy as jnp
from jax import lax
from jax.experimental import pallas as pl
from jax.experimental.pallas import tpu as pltpu
from jax.sharding import PartitionSpec as P

CAP = 32
F32, BF16 = jnp.float32, jnp.bfloat16
ROWS = (((0,), (0,)), ((), ()))
LAST = (((1,), (1,)), ((), ()))
VMEM = pl.BlockSpec(memory_space=pltpu.VMEM)
SMEM = pl.BlockSpec(memory_space=pltpu.SMEM)
ANY = pl.BlockSpec(memory_space=pl.ANY)
LIMIT = 40 << 20


def mm(a, b, dims=(((1,), (0,)), ((), ()))):
    return lax.dot_general(a, b, dims, preferred_element_type=F32)


def shape(dims, kind=BF16):
    return jax.ShapeDtypeStruct(tuple(dims), kind)


def params(limit=LIMIT):
    return pltpu.CompilerParams(vmem_limit_bytes=limit)


def cost(flops, nbytes, weigh=64):
    return pl.CostEstimate(flops=int(flops) // weigh, bytes_accessed=int(nbytes) // weigh, transcendentals=0)


def fetch(source, held, sem, parts):
    width = source.shape[1] // parts
    copies = []
    for i in range(parts):
        cols = pl.ds(i * width, width)
        copies.append(pltpu.make_async_copy(source.at[:, cols], held.at[:, cols], sem.at[i]))
        copies[-1].start()
    return copies


def pick_kernel(me, routes, probs, tokens, out_grad, sel_out, both, again, held, sem):
    _, n_dp, _, width = both.shape
    copies = fetch(tokens, held.at[0], sem.at[0], n_dp) + fetch(out_grad, held.at[1], sem.at[1], n_dp)
    n = tokens.shape[0]
    hits = routes[...] == 0
    coef = jnp.sum(jnp.where(hits, probs[...], 0.0), axis=0, keepdims=True)
    routed = jnp.sum(jnp.where(hits, 1.0, 0.0), axis=0, keepdims=True) > 0.5
    flags = jnp.broadcast_to(jnp.where(routed, 1.0, 0.0), (8, n))
    before = lax.broadcasted_iota(jnp.int32, (n, n), 0) <= lax.broadcasted_iota(jnp.int32, (n, n), 1)
    upto = mm(flags.astype(BF16), jnp.where(before, 1.0, 0.0).astype(BF16))[:1]
    count = jnp.sum(flags[:1], axis=1, keepdims=True)
    lane = lax.broadcasted_iota(jnp.int32, (1, n), 1).astype(F32)
    rank = jnp.where(routed, upto - 1.0, count + lane - upto)
    sel = rank == lax.broadcasted_iota(jnp.int32, (CAP, n), 0).astype(F32)
    scale = jnp.sum(jnp.where(sel, coef, 0.0), axis=1, keepdims=True)
    sel = jnp.where(sel, 1.0, 0.0).astype(BF16)
    sel_out[...] = sel
    for copy in copies:
        copy.wait()
    for k in range(n_dp):
        cols = pl.ds(pl.multiple_of((me[0] ^ k) * width, 128), width)
        both[0, k] = mm(sel, held[0, :, cols]).astype(BF16)
        both[1, k] = (scale * mm(sel, held[1, :, cols])).astype(BF16)
        again[:, k] = both[:, k]


def pick(me, tokens, routes, probs, out_grad, n_dp):
    n, d = tokens.shape
    return pl.pallas_call(
        pick_kernel,
        out_shape=(shape((CAP, n)),) + (shape((2, n_dp, CAP, d // n_dp)),) * 2,
        in_specs=[SMEM, VMEM, VMEM, ANY, ANY],
        out_specs=(VMEM,) * 3,
        scratch_shapes=[pltpu.VMEM((2, n, d), BF16), pltpu.SemaphoreType.DMA((2, n_dp))],
        compiler_params=params(60 << 20),
        cost_estimate=cost(4 * CAP * n * d, 5 * n * d),
    )(me, routes.T, probs.T, tokens, out_grad)


def after(x, *deps):
    def kernel(*refs):
        del refs

    return pl.pallas_call(
        kernel,
        out_shape=shape(x.shape, x.dtype),
        in_specs=[ANY] * (1 + len(deps)),
        out_specs=ANY,
        input_output_aliases={0: 0},
        compiler_params=params(1 << 20),
        cost_estimate=cost(0, 0),
    )(x, *deps)


def lay_kernel(count, deps, whole, *refs):
    blocks, rest, sem = refs[:count], list(refs[count + deps : -1]), refs[-1]
    copies = []
    at = 0
    for b in blocks:
        rows = pl.ds(at, b.shape[2])
        at += b.shape[2]
        if whole:
            copies.append((b, rest[0].at[:, :, rows]))
        for k, out in enumerate(rest[whole:], 1):
            copies.append((b.at[:, k], out.at[:, rows]))
    copies = [pltpu.make_async_copy(a, b, sem.at[i]) for i, (a, b) in enumerate(copies)]
    for copy in copies:
        copy.start()
    for copy in copies:
        copy.wait()


def lay(blocks, whole, deps=()):
    arrays, slices, _, width = blocks[0].shape
    rows = sum(b.shape[2] for b in blocks)
    cut = slices - 1
    outs = [shape((arrays, slices, rows, width))] * whole + [shape((arrays, rows, width))] * cut
    return pl.pallas_call(
        functools.partial(lay_kernel, len(blocks), len(deps), whole),
        out_shape=outs,
        in_specs=[ANY] * (len(blocks) + len(deps)),
        out_specs=[ANY] * len(outs),
        scratch_shapes=[pltpu.SemaphoreType.DMA((len(blocks) * (whole + cut),))],
        compiler_params=params(1 << 20),
        cost_estimate=cost(0, 4 * arrays * slices * rows * width),
    )(*blocks, *deps)


def pile_kernel(count, *refs):
    blocks, out, sem = refs[:count], refs[-2], refs[-1]
    copies = [pltpu.make_async_copy(b, out.at[i], sem.at[i]) for i, b in enumerate(blocks)]
    for copy in copies:
        copy.start()
    for copy in copies:
        copy.wait()


def pile(blocks, *deps):
    return pl.pallas_call(
        functools.partial(pile_kernel, len(blocks)),
        out_shape=shape((len(blocks),) + blocks[0].shape),
        in_specs=[ANY] * (len(blocks) + len(deps)),
        out_specs=ANY,
        scratch_shapes=[pltpu.SemaphoreType.DMA((len(blocks),))],
        compiler_params=params(1 << 20),
        cost_estimate=cost(0, 4 * len(blocks) * blocks[0].size),
    )(*blocks, *deps)


def gather_rows(me, i, parts, rows):
    at = 0
    for part in parts:
        _, n_dp, count, width = part.shape
        for k in range(n_dp):
            cols = pl.ds(pl.multiple_of((me[0] ^ k) * width, 128), width)
            rows[at : at + count, cols] = part[i, k]
        at += count


class Stream:
    def __init__(self, copies):
        self.copies = copies
        self.started = 0

    def start(self, upto):
        while self.started < min(upto, len(self.copies)):
            for copy in self.copies[self.started]:
                copy.start()
            self.started += 1

    def take(self, i):
        for copy in self.copies[i]:
            copy.wait()


def slab_kernel(count, sides, me, *refs):
    parts, refs = refs[:count], refs[count:]
    gw, uw, dw, out, mine, left, right, rows, gate, up, wide, tall, wide_sem, tall_sem = refs
    ff, piece = gw.shape[1], tall.shape[1]
    _, n_dp, _, width = parts[0].shape
    sub = 768 if width % 768 == 0 else width
    steps = width // sub
    forth, spans = [], []
    for k in range(n_dp):
        for s in range(steps):
            span = pl.ds(pl.multiple_of((me[0] ^ k) * width + s * sub, 128), sub)
            slot = len(forth) % 4
            spans.append(span)
            forth.append([
                pltpu.make_async_copy(w.at[span], wide.at[j, span], wide_sem.at[slot, j]) for j, w in enumerate((gw, uw))
            ])
    back = Stream([
        [pltpu.make_async_copy(dw.at[pl.ds(i * piece, piece)], tall.at[i % 2], tall_sem.at[i % 2])]
        for i in range(ff // piece)
    ])
    forth = Stream(forth)
    forth.start(1)
    gather_rows(me, 1, parts, rows)
    forth.start(3)
    for i, span in enumerate(spans):
        k, s = i // steps, i % steps
        forth.take(i)
        forth.start(i + 4)
        if i >= len(spans) - 5:
            back.start(min(2, i + 6 - len(spans)))
        some = jnp.concatenate([p[0, k, :, s * sub : (s + 1) * sub] for p in parts])
        for acc, j in ((gate, 0), (up, 1)):
            more = mm(some, wide[j, span])
            acc[...] = more if i == 0 else acc[...] + more
    g, u = gate[...], up[...]
    sig = jax.nn.sigmoid(g)
    act = g * sig
    gate[...] = act
    out[:, :ff] = (act * u).astype(BF16)
    up[...] = u * sig * (1.0 + g * (1.0 - sig))
    for i in range(ff // piece):
        at = i * piece
        cols = slice(at, at + piece)
        back.take(i)
        grad = mm(rows[...], tall[i % 2], LAST)
        out[:, ff + at : ff + at + piece] = (grad * up[:, cols]).astype(BF16)
        out[:, 2 * ff + at : 2 * ff + at + piece] = (grad * gate[:, cols]).astype(BF16)
        back.start(i + 3)
    d = wide.shape[1]
    tile = 512
    for i in range(d // tile):
        cols = slice(i * tile, (i + 1) * tile)
        half = slice(i * tile % (d // 2), i * tile % (d // 2) + tile)
        theirs = left if i * tile < d // 2 else right
        term = mm(out[:, ff : 2 * ff], wide[0, cols], LAST) + mm(out[:, 2 * ff :], wide[1, cols], LAST)
        at, to = 0, [0, 0]
        for side, size in sides:
            some = term[at : at + size].astype(BF16)
            if side == 0:
                mine[to[0] : to[0] + size, cols] = some
            else:
                theirs[to[1] : to[1] + size, half] = some
            at += size
            to[side] += size


def slab(me, parts, sides, gw, uw, dw, dep):
    sizes = [p.shape[2] for p in parts]
    rows, (d, ff) = sum(sizes), gw.shape
    n = len(parts) + 3

    def kernel(me, *refs):
        slab_kernel(len(parts), tuple(zip(sides, sizes)), me, *refs[:n], *refs[n + 1 :])

    return pl.pallas_call(
        kernel,
        out_shape=(
            shape((rows, 3 * ff)),
            shape((rows // 2, d)),
            shape((rows // 2, d // 2)),
            shape((rows // 2, d // 2)),
        ),
        in_specs=[SMEM] + [VMEM] * len(parts) + [ANY] * 4,
        out_specs=(VMEM,) * 4,
        scratch_shapes=[
            pltpu.VMEM((rows, d), BF16),
            pltpu.VMEM((rows, ff), F32),
            pltpu.VMEM((rows, ff), F32),
            pltpu.VMEM((2, d, ff), BF16),
            pltpu.VMEM((2, 256, d), BF16),
            pltpu.SemaphoreType.DMA((4, 2)),
            pltpu.SemaphoreType.DMA((2,)),
        ],
        compiler_params=params(42 << 20),
        cost_estimate=cost(10 * rows * gw.size, 6 * gw.size, 1),
    )(me, *parts, gw, uw, dw, dep)


def fold_kernel(mine, left, right, _, *outs):
    half = left.shape[1]
    for i, out in enumerate(outs):
        rows = slice(i * CAP, (i + 1) * CAP)
        for cols, theirs in ((slice(0, half), left), (slice(half, 2 * half), right)):
            out[:, cols] = (mine[rows, cols].astype(F32) + theirs[rows].astype(F32)).astype(BF16)


def fold(mine, left, right, dep):
    rows, d = mine.shape
    return pl.pallas_call(
        fold_kernel,
        out_shape=[shape((CAP, d))] * (rows // CAP),
        in_specs=[VMEM] * 3 + [ANY],
        out_specs=[VMEM] * (rows // CAP),
        compiler_params=params(16 << 20),
        cost_estimate=cost(0, 6 * rows * d),
    )(mine, left, right, dep)


def put_kernel(groups, sel, _, *refs):
    *parts, out = refs
    each = len(parts) // groups
    for g in range(groups):
        total = parts[g * each][...].astype(F32)
        for part in parts[g * each + 1 : (g + 1) * each]:
            total = total + part[...].astype(F32)
        width = total.shape[1]
        out[:, g * width : (g + 1) * width] = mm(sel[...], total.astype(BF16), ROWS).astype(BF16)


def put(sel, groups, dep):
    parts = [p for group in groups for p in group]
    d = sum(group[0].shape[1] for group in groups)
    return pl.pallas_call(
        functools.partial(put_kernel, len(groups)),
        out_shape=shape((sel.shape[1], d)),
        in_specs=[VMEM, ANY] + [VMEM] * len(parts),
        out_specs=VMEM,
        compiler_params=params(32 << 20),
        cost_estimate=cost(2 * sel.size * d, 4 * sel.size * d),
    )(sel, dep, *parts)


def contract_kernel(n_slices, n_grads, n_totals, *refs):
    slices, refs = refs[:n_slices], refs[n_slices:]
    grads, refs = refs[:n_grads], refs[n_grads:]
    totals, refs = refs[:n_totals], refs[n_totals:]
    outs, mark, (picked, scaled, rows) = refs[:3], refs[3], refs[4:]
    mark[...] = jnp.zeros(mark.shape, F32)

    @pl.when(pl.program_id(0) == 0)
    def _():
        at = 0
        for block in slices:
            size = block.shape[-2]
            whole = len(block.shape) == 4
            picked[at : at + size] = block[0, 0] if whole else block[0]
            scaled[at : at + size] = block[1, 0] if whole else block[1]
            at += size
        at = 0
        for block in grads:
            size = block.shape[0]
            rows[at : at + size] = block[...]
            at += size

    ff, tile = rows.shape[1] // 3, outs[0].shape[0]
    cols = pl.ds(pl.multiple_of(pl.program_id(0) * tile, tile), tile)

    def put_tile(n, value):
        if n_totals:
            value = value + totals[n][...].astype(F32)
        outs[n][...] = value.astype(outs[n].dtype)

    put_tile(0, mm(picked[:, cols], rows[:, ff : 2 * ff], ROWS))
    put_tile(1, mm(picked[:, cols], rows[:, 2 * ff :], ROWS))
    put_tile(2, mm(rows[:, :ff], scaled[:, cols], ROWS))


def contract(slices, grads, totals, tile=512):
    rows = sum(b.shape[0] for b in grads)
    width, ff = slices[0].shape[-1], grads[0].shape[1] // 3
    tile = tile if width % tile == 0 else 256
    outs = (shape((width, ff)), shape((width, ff)), shape((ff, width)))
    held = 2 * rows * (2 * width + 3 * ff)
    tall = pl.BlockSpec((tile, ff), lambda i: (i, 0))
    wide = pl.BlockSpec((ff, tile), lambda i: (0, i))
    return pl.pallas_call(
        functools.partial(contract_kernel, len(slices), len(grads), len(totals)),
        out_shape=(list(outs) if totals else [pltpu.VMEM(o.shape, o.dtype) for o in outs]) + [shape((8, 128), F32)],
        grid=(width // tile,),
        in_specs=[VMEM] * (len(slices) + len(grads)) + [tall, tall, wide][: len(totals)],
        out_specs=[tall, tall, wide, pl.BlockSpec((8, 128), lambda i: (0, 0))],
        scratch_shapes=[pltpu.VMEM((rows, width), BF16)] * 2 + [pltpu.VMEM((rows, 3 * ff), BF16)],
        compiler_params=params((42 if held < 16 << 20 else 56) << 20),
        cost_estimate=cost(6 * rows * width * ff, 2 * rows * (2 * width + 3 * ff) + 12 * width * ff, 1),
    )(*slices, *grads, *totals)


def on_device(tokens, routes, route_probs, gate_weight, up_weight, down_weight, out_grad):
    n_dp, n_fetch = lax.axis_size("dp"), lax.axis_size("fetch")
    chips = n_fetch // 2
    me = lax.axis_index("dp").astype(jnp.int32).reshape(1)

    def move(x, hop):
        pairs = [(2 * z + c, 2 * ((z + hop) % chips) + c) for z in range(chips) for c in range(2)]
        return lax.ppermute(x, "fetch", pairs)

    def swap(x):
        return lax.ppermute(x, "fetch", [(k, k ^ 1) for k in range(n_fetch)])

    def across(x, bits):
        return lax.ppermute(x, "dp", [(k, k ^ bits) for k in range(n_dp)])

    offsets = [0]
    for s in range(1, chips // 2 + 1):
        offsets += [-s] if 2 * s == chips else [-s, s]

    sel, own, again = pick(me, tokens, routes, route_probs, out_grad, n_dp)
    blocks = {0: own, -1: move(own, 1)}
    for s in range(2, chips // 2 + 1):
        blocks[-s] = move(blocks[1 - s], 1)
    for s in range(1, chips // 2):
        blocks[s] = move(after(again, blocks[-1]) if s == 1 else blocks[s - 1], -1)
    here, beside = [own, blocks[-1]], [blocks[o] for o in offsets[2:]]
    here_theirs = [swap(x) for x in here]
    near_cuts = lay(here, False, here_theirs[:1])
    near_got = [across(cut, k) for k, cut in enumerate(near_cuts, 1)]
    far, *far_cuts = lay(beside, True, near_got + here_theirs[1:])
    far_theirs = swap(far)
    far_got = [across(cut, k) for k, cut in enumerate(far_cuts, 1)]
    near_theirs = swap(pile(near_got))

    parts = here + [far] + here_theirs + [far_theirs]
    rows, mine, left, right = slab(me, parts, (0, 0, 0, 1, 1, 1), gate_weight, up_weight, down_weight, near_theirs)
    far_got_theirs = swap(pile(far_got, left))
    summed, *others = fold(mine, swap(after(left, *far_got)), swap(right), far_got_theirs)
    slices = [parts]
    for k in range(n_dp - 1):
        slices.append([near_got[k], far_got[k], near_theirs[k], far_got_theirs[k]])
    if n_dp == 4:
        half = rows.shape[0] // 2
        by_x, by_y = after(across(rows, 1), summed), after(across(rows, 2), summed)
        first = [rows, by_x, by_y]
        last = [across(by_x[:half], 2), across(by_y[half:], 1)]
    else:
        got = [across(rows, k) for k in range(1, n_dp)]
        first, last = [rows] + got[:-1], got[-1:]
    *totals, mark = contract(sum(slices[:-1], []), first, [])
    gate_grad, up_grad, down_grad, _ = contract(slices[-1], last, totals)
    token_grad = put(sel, [[summed] + [move(x, o) for x, o in zip(others, offsets[1:])]], mark)
    return token_grad, gate_grad, up_grad, down_grad


def solution(mesh):
    return jax.shard_map(
        on_device,
        mesh=mesh,
        in_specs=(
            P(("dp", "fetch"), None),
            P(("dp", "fetch"), None),
            P(("dp", "fetch"), None),
            P(None, "fetch"),
            P(None, "fetch"),
            P("fetch", None),
            P(("dp", "fetch"), None),
        ),
        out_specs=(P(("dp", "fetch"), None), P("dp", "fetch"), P("dp", "fetch"), P("fetch", "dp")),
        check_vma=False,
    )
```
